32 devices in a mesh: grp: 2 (over y), gy: 4 (over z), ch: 2 (over x), gx: 2 (over core).
Axes of the slice: x: 2, y: 2, z: 4, core: 2. Of those that a mesh axis runs over, the one named last changes fastest.
Arguments:
- activations: bfloat16 [384, 4, 8, 256], P('ch', 'grp', 'gy', 'gx'), parts along dimension 1, may hold values from -6 to 6
- weight: bfloat16 [27, 384, 384], P(None, 'ch'), may hold values from -0.0625 to 0.0625
- cotangent: bfloat16 [384, 4, 8, 256], P('ch', 'grp', 'gy', 'gx'), parts along dimension 1, may hold values from -6 to 6
- shear_shift: int32 [2], P('grp'), parts along dimension 0, may hold values from 0 to 255
Outputs:
- features: bfloat16 [384, 4, 8, 256], P('ch', 'grp', 'gy', 'gx'), parts along dimension 1
- input_grad: bfloat16 [384, 4, 8, 256], P('ch', 'grp', 'gy', 'gx'), parts along dimension 1
- weight_grad: float32 [54, 384, 384], P('grp', 'ch'), parts along dimension 0
The draws below stay inside these ranges and needn't reach their ends.
There are 2 independent parts, one for each index of `grp`. The reference program is written for one: setup_inputs(seed, part) draws one part's arguments, and reference() takes and returns one part's arrays. A program takes and returns all parts, laid end to end along the dimension named above; an argument that names none is the same for every part. Nothing has to cross between parts.
Inputs may be any that keep to these rules, and one draw needn't show every extreme that they name: `shear_shift`: one offset for the group's snapshot.
All inputs are finite; a program needn't handle non-finite values.
Results may differ from the reference program's by a relative error of at most 0.001.
Values may be sent and summed in bfloat16 or wider, within the bound.
A program may use at most 128 MiB of HBM per device.

```python
import jax
import jax.numpy as jnp

C = 384
Z = 2
NY = 8
NX = 256


def shard_levels(own_key, shape, pieces, smallest, top_value):
    def one(position, parts):
        heights = jax.random.uniform(jax.random.fold_in(jax.random.fold_in(own_key, 6), position), (parts,), jnp.float32, smallest / len(pieces), top_value / len(pieces))
        return jnp.repeat(jnp.exp(heights), shape[position] // parts).reshape((-1,) + (1,) * (len(shape) - position - 1))

    loudness = one(*pieces[0])
    for cut in pieces[1:]:
        loudness = loudness * one(*cut)
    return loudness


def gaussian(stream_key, extent, deviation, bound, cuts=(), held_as=jnp.bfloat16):
    gain = shard_levels(stream_key, extent, cuts, -0.22, 0.18) if cuts else 1.0
    result = jax.random.normal(stream_key, extent, jnp.float32) * deviation * gain
    return jnp.minimum(jnp.maximum(result, -bound), bound).astype(held_as)


def setup_inputs(seed: int = 0, part: int = 0) -> dict:
    seeds = jax.random.split(jax.random.key(seed), 5)
    own_keys = jax.random.split(jax.random.fold_in(seeds[4], part), 5)
    return {
        "activations": gaussian(own_keys[0], (C, Z, NY, NX), 1.0, 6.0, ((0, 2), (2, 4), (3, 2))),
        "weight": gaussian(seeds[1], (27, C, C), (27 * C) ** -0.5, 0.0625, ((1, 2),)),
        "cotangent": gaussian(own_keys[2], (C, Z, NY, NX), 1.0, 6.0, ((0, 2), (2, 4), (3, 2))),
        "shear_shift": jax.random.randint(own_keys[3], (1,), 0, NX).astype(jnp.int32),
    }


def extend(field, shift_value):
    below = jnp.roll(field[:, :, -1:], shift_value, axis=3)
    above = jnp.roll(field[:, :, :1], -shift_value, axis=3)
    padded = jnp.concatenate([below, field, above], 2)
    padded = jnp.concatenate([padded[..., -1:], padded, padded[..., :1]], 3)
    return jnp.pad(padded, ((0, 0), (1, 1), (0, 0), (0, 0)))

def convolve(extended, kernel):
    planes = extended.shape[1] - 2
    y_cells = extended.shape[2] - 2
    x_cells = extended.shape[3] - 2
    total = jnp.zeros((kernel.shape[1], planes, y_cells, x_cells), kernel.dtype)
    for z_step in range(3):
        for y_step in range(3):
            for x_step in range(3):
                window = extended[:, z_step:z_step + planes, y_step:y_step + y_cells, x_step:x_step + x_cells]
                total = total + jnp.einsum('oi,izyx->ozyx', kernel[9 * z_step + 3 * y_step + x_step], window)
    return total

def reference(activations, weight, cotangent, shear_shift):
    shift_value = shear_shift[0]

    def layer(inputs, kernel):
        return convolve(extend(inputs, shift_value), kernel)
    output, pullback = jax.vjp(layer, activations.astype(jnp.float32), weight.astype(jnp.float32))
    grad_in, grad_kernel = pullback(cotangent.astype(jnp.float32))
    scale = float(Z * NY * NX) ** (-0.5)
    return (output.astype(jnp.bfloat16), grad_in.astype(jnp.bfloat16), grad_kernel * scale)
```

```python
import functools

import jax
import jax.numpy as jnp
from jax import lax
from jax.experimental import pallas as pl
from jax.experimental.pallas import tpu as pltpu
from jax.sharding import PartitionSpec as P

BF16 = jnp.bfloat16
F32 = jnp.float32
LIMIT = 56 * 1024 * 1024


def gather_kernel(n, nch, a_ref, t_ref, buf, loc_sem, zs_sem, zr_sem, xs_sem, xr_sem, cs_sem, cr_sem):
    q = lax.axis_index("gy")
    h = lax.axis_index("ch")
    c = lax.axis_index("gx")
    other = 1 - c

    barrier = pltpu.get_barrier_semaphore()

    @pl.when(q > 0)
    def _():
        pl.semaphore_signal(barrier, inc=1, device_id={"gy": q - 1}, device_id_type=pl.DeviceIdType.MESH)

    @pl.when(q < n - 1)
    def _():
        pl.semaphore_signal(barrier, inc=1, device_id={"gy": q + 1}, device_id_type=pl.DeviceIdType.MESH)

    for d in range(1, nch):
        pl.semaphore_signal(
            barrier, inc=1, device_id={"ch": lax.rem(h + d, nch)}, device_id_type=pl.DeviceIdType.MESH
        )
    pl.semaphore_signal(barrier, inc=1, device_id={"gx": other}, device_id_type=pl.DeviceIdType.MESH)
    own_a = pltpu.make_async_copy(a_ref, buf.at[q, c, h], loc_sem.at[0])
    own_t = pltpu.make_async_copy(t_ref, buf.at[q, c, nch], loc_sem.at[1])
    own_a.start()
    own_t.start()
    own_a.wait()
    own_t.wait()
    edges = jnp.where(q > 0, 1, 0) + jnp.where(q < n - 1, 1, 0)
    pl.semaphore_wait(barrier, edges + nch)

    def z_copy(step, direction, kind, source):
        slot = buf.at[source, c, h if kind == 0 else nch]
        return pltpu.make_async_remote_copy(
            src_ref=slot,
            dst_ref=slot,
            send_sem=zs_sem.at[direction, step, kind],
            recv_sem=zr_sem.at[direction, step, kind],
            device_id={"gy": q - 1 if direction == 0 else q + 1},
            device_id_type=pl.DeviceIdType.MESH,
        )

    def x_copy(source, d):
        slot = buf.at[source, c, h]
        return pltpu.make_async_remote_copy(
            src_ref=slot,
            dst_ref=slot,
            send_sem=xs_sem.at[source, d],
            recv_sem=xr_sem.at[source, d],
            device_id={"ch": lax.rem(h + d, nch)},
            device_id_type=pl.DeviceIdType.MESH,
        )

    def x_arrival(source, d):
        slot = buf.at[source, c, lax.rem(h - d + nch, nch)]
        return pltpu.make_async_remote_copy(
            src_ref=slot,
            dst_ref=slot,
            send_sem=xs_sem.at[source, d],
            recv_sem=xr_sem.at[source, d],
            device_id={"ch": lax.rem(h + d, nch)},
            device_id_type=pl.DeviceIdType.MESH,
        )

    def c_copy(source, d, side):
        kind = nch if d == nch else lax.rem(h - d + nch, nch)
        slot = buf.at[source, side, kind]
        return pltpu.make_async_remote_copy(
            src_ref=slot,
            dst_ref=slot,
            send_sem=cs_sem.at[source, d],
            recv_sem=cr_sem.at[source, d],
            device_id={"gx": other},
            device_id_type=pl.DeviceIdType.MESH,
        )

    def forward(source):
        for d in range(1, nch):
            x_copy(source, d).start()
        c_copy(source, 0, c).start()
        c_copy(source, nch, c).start()

    def relay(source):
        for d in range(1, nch):
            x_arrival(source, d).wait_recv()
            c_copy(source, d, c).start()

    for step in range(n - 1):
        down = (q >= 1) & (q + step < n)
        up = (q + 1 < n) & (q - step >= 0)

        @pl.when(down)
        def _():
            for kind in range(2):
                z_copy(step, 0, kind, q + step).start()

        @pl.when(up)
        def _():
            for kind in range(2):
                z_copy(step, 1, kind, q - step).start()

        if step == 0:
            forward(q)
            relay(q)
        else:

            @pl.when(q + step < n)
            def _():
                forward(q + step)
                relay(q + step)

            @pl.when(q - step >= 0)
            def _():
                forward(q - step)
                relay(q - step)

        @pl.when(q + step + 1 < n)
        def _():
            for kind in range(2):
                z_copy(step, 0, kind, q + step + 1).wait_recv()

        @pl.when(q - step - 1 >= 0)
        def _():
            for kind in range(2):
                z_copy(step, 1, kind, q - step - 1).wait_recv()

    @pl.when(q == 0)
    def _():
        forward(q + n - 1)
        relay(q + n - 1)

    @pl.when(q == n - 1)
    def _():
        forward(q - (n - 1))
        relay(q - (n - 1))

    for step in range(n - 1):

        @pl.when((q >= 1) & (q + step < n))
        def _():
            for kind in range(2):
                z_copy(step, 0, kind, q + step).wait_send()

        @pl.when((q + 1 < n) & (q - step >= 0))
        def _():
            for kind in range(2):
                z_copy(step, 1, kind, q - step).wait_send()

    for source in range(n):
        for d in range(1, nch):
            x_copy(source, d).wait_send()
        for d in range(nch + 1):
            c_copy(source, d, c).wait_send()
            c_copy(source, d, other).wait_recv()


def gather(n, nch, mine_a, mine_t):
    pieces, local_ch, x_cells = mine_a.shape
    return pl.pallas_call(
        functools.partial(gather_kernel, n, nch),
        out_shape=jax.ShapeDtypeStruct((n, 2, nch + 1, pieces, local_ch, x_cells), BF16),
        in_specs=[pl.BlockSpec(memory_space=pltpu.VMEM)] * 2,
        out_specs=pl.BlockSpec(memory_space=pltpu.VMEM),
        scratch_shapes=[
            pltpu.SemaphoreType.DMA((2,)),
            pltpu.SemaphoreType.DMA((2, n, 2)),
            pltpu.SemaphoreType.DMA((2, n, 2)),
            pltpu.SemaphoreType.DMA((n, nch)),
            pltpu.SemaphoreType.DMA((n, nch)),
            pltpu.SemaphoreType.DMA((n, nch + 1)),
            pltpu.SemaphoreType.DMA((n, nch + 1)),
        ],
        compiler_params=pltpu.CompilerParams(
            collective_id=0, has_side_effects=True, vmem_limit_bytes=LIMIT
        ),
        name="gather_fields",
    )(mine_a, mine_t)


def local_kernel(n, nch, yl, scale, place, buf, w_ref, near, turn, f_ref, g_ref, wg_ref, ext, rolled, ax, tx):
    local_ch = w_ref.shape[1]
    amount = w_ref.shape[2]
    x_cells = buf.shape[-1]
    row = 2 * x_cells
    q = place[0]
    ny = n * yl
    plane = (ny + 2) * row
    flat = ny * row

    for r in range(yl + 2):
        if r == 0:
            source, y, side = lax.rem(q + n - 1, n), yl - 1, 0
        elif r == yl + 1:
            source, y, side = lax.rem(q + 1, n), 0, 2
        else:
            source, y, side = q, r - 1, 1
        for z in range(2):
            at = (z * (yl + 2) + r) * x_cells
            for field, out, size in ((0, ax, amount), (1, tx, local_ch)):
                halves = [
                    buf[source, k, :nch, z * yl + y].reshape(amount, x_cells)
                    if field == 0
                    else buf[source, k, nch, z * yl + y]
                    for k in range(2)
                ]
                for c in range(3):
                    moved = jnp.dot(
                        halves[0], near[side, c, :x_cells], preferred_element_type=F32
                    ) + jnp.dot(halves[1], near[side, c, x_cells:], preferred_element_type=F32)
                    out[c, :, at : at + x_cells] = moved.astype(BF16)

    width = yl * x_cells
    span = (yl + 2) * x_cells
    valid = [(a, z, z + a - 1) for a in range(3) for z in range(2) if 0 <= z + a - 1 < 2]

    def features_step(b, carry):
        out = list(carry)
        for a, z, zz in valid:
            for c in range(3):
                window = ax[c, :, pl.ds(pl.multiple_of(zz * span + b * x_cells, x_cells), width)]
                out[z] += jnp.dot(w_ref[9 * a + 3 * b + c], window, preferred_element_type=F32)
        return tuple(out)

    planes = lax.fori_loop(0, 3, features_step, (jnp.zeros((local_ch, width), F32),) * 2)
    for z in range(2):
        f_ref[:, z * width : (z + 1) * width] = planes[z].astype(BF16)

    def grad_step(b, carry):
        out = list(carry)
        for a, z, _ in valid:
            for c in range(3):
                zz = z + a - 1
                window = tx[c, :, pl.ds(pl.multiple_of(zz * span + b * x_cells, x_cells), width)]
                out[z] += lax.dot_general(
                    w_ref[9 * (2 - a) + 3 * (2 - b) + 2 - c],
                    window,
                    (((0,), (0,)), ((), ())),
                    preferred_element_type=F32,
                )
        return tuple(out)

    planes = lax.fori_loop(0, 3, grad_step, (jnp.zeros((amount, width), F32),) * 2)
    for z in range(2):
        g_ref[:, z * width : (z + 1) * width] = planes[z]

    @pl.loop(0, n)
    def _(source):
        for z in range(2):
            for y in range(yl):
                at = pl.multiple_of(z * plane + (1 + source * yl + y) * row, row)
                to = pl.multiple_of(z * flat + (source * yl + y) * row, row)
                for k in range(2):
                    ext[:, pl.ds(at + k * x_cells, x_cells)] = buf[source, k, :nch, z * yl + y].reshape(
                        amount, x_cells
                    )
                    rolled[1, :, pl.ds(to + k * x_cells, x_cells)] = buf[source, k, nch, z * yl + y]
                line = rolled[1, :, pl.ds(to, row)]
                for c in (0, 2):
                    rolled[c, :, pl.ds(to, row)] = jnp.dot(
                        line, turn[c], preferred_element_type=F32
                    ).astype(BF16)

    for z in range(2):
        first = ext[:, z * plane + row : z * plane + 2 * row]
        last = ext[:, z * plane + ny * row : z * plane + (ny + 1) * row]
        ext[:, z * plane : z * plane + row] = jnp.dot(
            last, turn[3], preferred_element_type=F32
        ).astype(BF16)
        ext[:, z * plane + (ny + 1) * row : (z + 1) * plane] = jnp.dot(
            first, turn[4], preferred_element_type=F32
        ).astype(BF16)

    def weight_step(b, carry):
        for a in range(3):
            total = None
            for a_of, z, zz in valid:
                if a_of != a:
                    continue
                left = rolled[:, :, z * flat : (z + 1) * flat].reshape(3 * local_ch, flat)
                right = ext[:, pl.ds(pl.multiple_of(zz * plane + b * row, row), flat)]
                part = lax.dot_general(
                    left, right, (((1,), (1,)), ((), ())), preferred_element_type=F32
                )
                total = part if total is None else total + part
            wg_ref[pl.ds(9 * a + 3 * b, 3)] = (total * scale).reshape(3, local_ch, amount)
        return carry

    lax.fori_loop(0, 3, weight_step, 0)


def shift_matrix(full, offset, begin, count):
    source = (lax.broadcasted_iota(jnp.int32, (full, count), 1) + begin + offset) % full
    return (lax.broadcasted_iota(jnp.int32, (full, count), 0) == source).astype(BF16)


def on_device(activations, weight, cotangent, shear_shift):
    local_ch, planes, yl, x_cells = activations.shape
    n = lax.axis_size("gy")
    nch = lax.axis_size("ch")
    amount = weight.shape[2]
    full = 2 * x_cells
    q = lax.axis_index("gy")
    shift = shear_shift[0]
    scale = float(planes * yl * n * full) ** (-0.5)

    mine_a = activations.reshape(local_ch, planes * yl, x_cells).transpose(1, 0, 2)
    mine_t = cotangent.reshape(local_ch, planes * yl, x_cells).transpose(1, 0, 2)
    buf = gather(n, nch, mine_a, mine_t)

    begin = lax.axis_index("gx") * x_cells
    below = jnp.where(q == 0, -shift, 0)
    above = jnp.where(q == n - 1, shift, 0)
    near = jnp.stack(
        [
            jnp.stack([shift_matrix(full, ghost + c - 1, begin, x_cells) for c in range(3)])
            for ghost in (below, 0, above)
        ]
    )
    turn = jnp.stack([shift_matrix(full, offset, 0, full) for offset in (1, 0, -1, -shift, shift)])
    ny = n * yl
    vmem = pl.BlockSpec(memory_space=pltpu.VMEM)
    features, term, weight_grad = pl.pallas_call(
        functools.partial(local_kernel, n, nch, yl, scale),
        out_shape=(
            jax.ShapeDtypeStruct((local_ch, planes * yl * x_cells), BF16),
            jax.ShapeDtypeStruct((amount, planes * yl * x_cells), F32),
            jax.ShapeDtypeStruct((27, local_ch, amount), F32),
        ),
        in_specs=[pl.BlockSpec(memory_space=pltpu.SMEM), vmem, vmem, vmem, vmem],
        out_specs=(vmem, vmem, vmem),
        scratch_shapes=[
            pltpu.VMEM((amount, planes * (ny + 2) * full), BF16),
            pltpu.VMEM((3, local_ch, planes * ny * full), BF16),
            pltpu.VMEM((3, amount, planes * (yl + 2) * x_cells), BF16),
            pltpu.VMEM((3, local_ch, planes * (yl + 2) * x_cells), BF16),
        ],
        compiler_params=pltpu.CompilerParams(vmem_limit_bytes=LIMIT),
        name="local_sums",
    )(q.astype(jnp.int32).reshape(1), buf, weight, near, turn)
    grad_in = lax.psum_scatter(term, "ch", scatter_dimension=0, tiled=True)
    shape = (local_ch, planes, yl, x_cells)
    return (features.reshape(shape), grad_in.astype(BF16).reshape(shape), weight_grad)


def solution(mesh):
    return jax.shard_map(
        on_device,
        mesh=mesh,
        in_specs=(
            P("ch", "grp", "gy", "gx"),
            P(None, "ch", None),
            P("ch", "grp", "gy", "gx"),
            P("grp"),
        ),
        out_specs=(P("ch", "grp", "gy", "gx"), P("ch", "grp", "gy", "gx"), P("grp", "ch", None)),
        check_vma=False,
    )
```

```python
import functools

import jax
import jax.numpy as jnp
from jax import lax
from jax.experimental import pallas as pl
from jax.experimental.pallas import tpu as pltpu
from jax.sharding import PartitionSpec as P

BF16 = jnp.bfloat16
F32 = jnp.float32
LIMIT = 56 * 1024 * 1024

MESH = pl.DeviceIdType.MESH


def layer_kernel(
    n, nch, yl, scale,
    a_ref, t_ref, w_ref, near, turn,
    f_ref, g_ref, wg_ref,
    buf, ext, rolled, ax, tx, term, arrived,
    loc_sem, zs_sem, zr_sem, hs_sem, hr_sem, xs_sem, xr_sem, cs_sem, cr_sem, gs_sem, gr_sem,
):
    q = lax.axis_index("gy")
    h = lax.axis_index("ch")
    c = lax.axis_index("gx")
    other = 1 - c
    local_ch = w_ref.shape[1]
    amount = w_ref.shape[2]
    x_cells = buf.shape[-1]
    row = 2 * x_cells
    ny = n * yl
    plane = (ny + 2) * row
    flat = ny * row
    width = yl * x_cells
    span = (yl + 2) * x_cells
    valid = [(a, z, z + a - 1) for a in range(3) for z in range(2) if 0 <= z + a - 1 < 2]

    whole = (0, 2 * yl)
    halo = {"bottom": (2 * yl - 2, 2), "top": (0, 2)}
    rest = {"bottom": (0, 2 * yl - 2), "top": (2, 2 * yl - 2)}
    ends = {"bottom": (q == 0, n - 1), "top": (q == n - 1, 0)}

    def copy(slot, to, send, recv):
        return pltpu.make_async_remote_copy(
            src_ref=slot, dst_ref=slot, send_sem=send, recv_sem=recv, device_id=to, device_id_type=MESH
        )

    def channel(kind):
        return h if kind == 0 else nch

    def z_copy(step, direction, kind, source, part=whole):
        return copy(
            buf.at[source, c, channel(kind), pl.ds(*part)],
            {"gy": q - 1 if direction == 0 else q + 1},
            zs_sem.at[direction, step, kind],
            zr_sem.at[direction, step, kind],
        )

    def h_copy(kind, source, part, to):
        return copy(
            buf.at[source, c, channel(kind), pl.ds(*part)], {"gy": to}, hs_sem.at[kind], hr_sem.at[kind]
        )

    def x_copy(source, d, part=whole, sub=0, arrival=False):
        panel = lax.rem(h - d + nch, nch) if arrival else h
        return copy(
            buf.at[source, c, panel, pl.ds(*part)],
            {"ch": lax.rem(h + d, nch)},
            xs_sem.at[source, d, sub],
            xr_sem.at[source, d, sub],
        )

    def c_copy(source, d, part=whole, sub=0, side=None):
        kind = nch if d == nch else lax.rem(h - d + nch, nch)
        return copy(
            buf.at[source, c if side is None else side, kind, pl.ds(*part)],
            {"gx": other},
            cs_sem.at[source, d, sub],
            cr_sem.at[source, d, sub],
        )

    def pass_on(source, kind, part=whole, sub=0):
        if kind == 0:
            for d in range(1, nch):
                x_copy(source, d, part, sub).start()
            c_copy(source, 0, part, sub).start()
        else:
            c_copy(source, nch, part, sub).start()

    def relay(source, part=whole, sub=0):
        for d in range(1, nch):
            x_copy(source, d, part, sub, True).wait_recv()
            c_copy(source, d, part, sub).start()

    def from_core(source, kinds, part=whole, sub=0):
        for d in kinds:
            c_copy(source, d, part, sub, other).wait_recv()

    fields = range(nch)

    def each(step, body):
        if step < n - 1:

            @pl.when(q + step < n)
            def _():
                body(0, q + step, whole)

            @pl.when(q - step >= 0)
            def _():
                body(1, q - step, whole)
        else:
            for direction, name in ((0, "bottom"), (1, "top")):

                @pl.when(ends[name][0])
                def _(direction=direction, name=name):
                    body(direction, ends[name][1], rest[name])

    def onward(step, direction, kind, source):
        def go(part):
            z_copy(step, direction, kind, source, part).start()

        last = step == n - 2
        if direction == 0:

            @pl.when(q >= 1)
            def _():
                go(rest["bottom"] if last else whole)
        else:

            @pl.when(q < n - 1)
            def _():
                go(rest["top"] if last else whole)

    barrier = pltpu.get_barrier_semaphore()

    def greet(to):
        pl.semaphore_signal(barrier, inc=1, device_id=to, device_id_type=MESH)

    @pl.when(q > 0)
    def _():
        greet({"gy": q - 1})

    @pl.when(q < n - 1)
    def _():
        greet({"gy": q + 1})

    for name in ("bottom", "top"):

        @pl.when(ends[name][0])
        def _(name=name):
            greet({"gy": ends[name][1]})

    for d in range(1, nch):
        greet({"ch": lax.rem(h + d, nch)})
    greet({"gx": other})
    own_a = pltpu.make_async_copy(a_ref, buf.at[q, c, h], loc_sem.at[0])
    own_t = pltpu.make_async_copy(t_ref, buf.at[q, c, nch], loc_sem.at[1])
    own_a.start()
    own_t.start()
    own_a.wait()
    own_t.wait()
    pl.semaphore_wait(barrier, 2 + nch)

    for kind in (1, 0):

        @pl.when(q == 0)
        def _(kind=kind):
            h_copy(kind, 0, halo["top"], n - 1).start()

        @pl.when(q == n - 1)
        def _(kind=kind):
            h_copy(kind, n - 1, halo["bottom"], 0).start()

    for kind in range(2):
        for direction in range(2):
            onward(0, direction, kind, q)
        pass_on(q, kind)

    def take(step):
        for kind in range(2):

            def body(direction, source, part, kind=kind):
                z_copy(step - 1, direction, kind, source, part).wait_recv()
                if step < n - 1:
                    onward(step, direction, kind, source)
                pass_on(source, kind, part)

            each(step, body)

    take(1)
    for name in ("bottom", "top"):

        @pl.when(ends[name][0])
        def _(name=name):
            source, part = ends[name][1], halo[name]
            for kind in (1, 0):
                h_copy(kind, source, part, source).wait_recv()
                pass_on(source, kind, part, 1)

    relay(q)

    from_core(q, (nch,))
    each(1, lambda direction, source, part: from_core(source, (nch,), part))
    for name in ("bottom", "top"):

        @pl.when(ends[name][0])
        def _(name=name):
            from_core(ends[name][1], (nch,), halo[name], 1)

    def surround(field):
        out = ax if field == 0 else tx
        for r in range(yl + 2):
            if r == 0:
                source, y, side = lax.rem(q + n - 1, n), yl - 1, 0
            elif r == yl + 1:
                source, y, side = lax.rem(q + 1, n), 0, 2
            else:
                source, y, side = q, r - 1, 1
            for z in range(2):
                at = (z * (yl + 2) + r) * x_cells
                halves = [
                    buf[source, k, :nch, 2 * y + z].reshape(amount, x_cells)
                    if field == 0
                    else buf[source, k, nch, 2 * y + z]
                    for k in range(2)
                ]
                for s in range(3):
                    moved = jnp.dot(
                        halves[0], near[side, s, :x_cells], preferred_element_type=F32
                    ) + jnp.dot(halves[1], near[side, s, x_cells:], preferred_element_type=F32)
                    out[s, :, at : at + x_cells] = moved.astype(BF16)

    surround(1)

    def grad_step(b, carry):
        out = list(carry)
        for a, z, zz in valid:
            for s in range(3):
                window = tx[s, :, pl.ds(pl.multiple_of(zz * span + b * x_cells, x_cells), width)]
                out[z] += lax.dot_general(
                    w_ref[9 * (2 - a) + 3 * (2 - b) + 2 - s],
                    window,
                    (((0,), (0,)), ((), ())),
                    preferred_element_type=F32,
                )
        return tuple(out)

    planes = lax.fori_loop(0, 3, grad_step, (jnp.zeros((amount, width), F32),) * 2)
    for z in range(2):
        term[:, :, z * width : (z + 1) * width] = planes[z].reshape(nch, local_ch, width)

    each(1, lambda direction, source, part: relay(source, part))
    for name in ("bottom", "top"):

        @pl.when(ends[name][0])
        def _(name=name):
            relay(ends[name][1], halo[name], 1)

    def g_copy(d):
        to = lax.rem(h + d, nch)
        return pltpu.make_async_remote_copy(
            src_ref=term.at[to],
            dst_ref=arrived.at[d],
            send_sem=gs_sem.at[d],
            recv_sem=gr_sem.at[d],
            device_id={"ch": to},
            device_id_type=MESH,
        )

    for step in range(2, n - 1):
        take(step)
        if step == 2:
            for d in range(1, nch):
                g_copy(d).start()
        if step > 2:
            each(step - 1, lambda direction, source, part: relay(source, part))

    from_core(q, fields)
    each(1, lambda direction, source, part: from_core(source, fields, part))
    for name in ("bottom", "top"):

        @pl.when(ends[name][0])
        def _(name=name):
            from_core(ends[name][1], fields, halo[name], 1)

    surround(0)

    def features_step(b, carry):
        out = list(carry)
        for a, z, zz in valid:
            for s in range(3):
                window = ax[s, :, pl.ds(pl.multiple_of(zz * span + b * x_cells, x_cells), width)]
                out[z] += jnp.dot(w_ref[9 * a + 3 * b + s], window, preferred_element_type=F32)
        return tuple(out)

    planes = lax.fori_loop(0, 3, features_step, (jnp.zeros((local_ch, width), F32),) * 2)
    for z in range(2):
        f_ref[:, z * width : (z + 1) * width] = planes[z].astype(BF16)

    if n > 3:
        each(n - 2, lambda direction, source, part: relay(source, part))
    for step in range(2, n - 1):
        each(
            step, lambda direction, source, part: from_core(source, range(nch + 1), part)
        )

    late = jnp.where(2 * q < n, n - 1, 0)
    base = jnp.where(2 * q < n, 0, 1)

    def lay_out(source):
        for z in range(2):
            for y in range(yl):
                at = pl.multiple_of(z * plane + (1 + source * yl + y) * row, row)
                to = pl.multiple_of(z * flat + (source * yl + y) * row, row)
                for k in range(2):
                    ext[:, pl.ds(at + k * x_cells, x_cells)] = buf[source, k, :nch, 2 * y + z].reshape(
                        amount, x_cells
                    )
                    rolled[1, :, pl.ds(to + k * x_cells, x_cells)] = buf[source, k, nch, 2 * y + z]
                line = rolled[1, :, pl.ds(to, row)]
                for s in (0, 2):
                    rolled[s, :, pl.ds(to, row)] = jnp.dot(
                        line, turn[s], preferred_element_type=F32
                    ).astype(BF16)

    @pl.loop(0, n - 1)
    def _(k):
        lay_out(base + k)

    def products(a, b, start, rows):
        total = None
        for a_of, z, zz in valid:
            if a_of != a:
                continue
            left = rolled[:, :, pl.ds(pl.multiple_of(z * flat + start * row, row), rows * row)]
            right = ext[:, pl.ds(pl.multiple_of(zz * plane + (start + b) * row, row), rows * row)]
            part = lax.dot_general(
                left.reshape(3 * local_ch, rows * row),
                right,
                (((1,), (1,)), ((), ())),
                preferred_element_type=F32,
            )
            total = part if total is None else total + part
        return (total * scale).reshape(3, local_ch, amount)

    def early(a):
        many = (n - 1) * yl
        first = base * yl
        for b in range(3):
            at = 9 * a + 3 * b
            if b == 1:
                wg_ref[at : at + 3] = products(a, b, first, many)
            else:
                wg_ref[at : at + 3] = products(a, b, first + (1 if b == 0 else 0), many - 1)

    early(0)
    early(2)
    take(n - 1)
    early(1)
    each(n - 1, lambda direction, source, part: relay(source, part))
    for d in range(1, nch):
        g_copy(d).wait_recv()
    total = term[h]
    for d in range(1, nch):
        total = total + arrived[d]
    g_ref[...] = total.astype(BF16)
    each(n - 1, lambda direction, source, part: from_core(source, range(nch + 1), part))

    lay_out(late)
    for z in range(2):
        first = ext[:, z * plane + row : z * plane + 2 * row]
        last = ext[:, z * plane + ny * row : z * plane + (ny + 1) * row]
        ext[:, z * plane : z * plane + row] = jnp.dot(
            last, turn[3], preferred_element_type=F32
        ).astype(BF16)
        ext[:, z * plane + (ny + 1) * row : (z + 1) * plane] = jnp.dot(
            first, turn[4], preferred_element_type=F32
        ).astype(BF16)

    for a in range(3):
        for b in range(3):
            at = 9 * a + 3 * b
            more = products(a, b, late * yl, yl)
            if b == 0:
                more = more + products(a, b, lax.rem(late * yl + yl, ny), 1)
            if b == 2:
                more = more + products(a, b, lax.rem(late * yl + ny - 1, ny), 1)
            wg_ref[at : at + 3] += more

    for step in range(n - 1):
        for kind in range(2):
            last = step == n - 2

            @pl.when((q >= 1) & (q + step < n))
            def _():
                z_copy(step, 0, kind, q + step, rest["bottom"] if last else whole).wait_send()

            @pl.when((q < n - 1) & (q - step >= 0))
            def _():
                z_copy(step, 1, kind, q - step, rest["top"] if last else whole).wait_send()

    def gone(source, part=whole, sub=0):
        for d in range(1, nch):
            x_copy(source, d, part, sub).wait_send()
        for d in range(nch + 1):
            c_copy(source, d, part, sub).wait_send()

    gone(q)
    for step in range(1, n):
        each(step, lambda direction, source, part: gone(source, part))
    for name, mine in (("bottom", "top"), ("top", "bottom")):

        @pl.when(ends[name][0])
        def _(name=name, mine=mine):
            gone(ends[name][1], halo[name], 1)
            for kind in range(2):
                h_copy(kind, q, halo[mine], ends[name][1]).wait_send()

    for d in range(1, nch):
        g_copy(d).wait_send()


def shift_matrix(full, offset, begin, count):
    source = (lax.broadcasted_iota(jnp.int32, (full, count), 1) + begin + offset) % full
    return (lax.broadcasted_iota(jnp.int32, (full, count), 0) == source).astype(BF16)


def on_device(activations, weight, cotangent, shear_shift):
    local_ch, planes, yl, x_cells = activations.shape
    n = lax.axis_size("gy")
    nch = lax.axis_size("ch")
    amount = weight.shape[2]
    full = 2 * x_cells
    ny = n * yl
    q = lax.axis_index("gy")
    shift = shear_shift[0]
    scale = float(planes * ny * full) ** (-0.5)

    def pieces(field):
        return field.transpose(2, 1, 0, 3).reshape(planes * yl, local_ch, x_cells)

    begin = lax.axis_index("gx") * x_cells
    below = jnp.where(q == 0, -shift, 0)
    above = jnp.where(q == n - 1, shift, 0)
    near = jnp.stack(
        [
            jnp.stack([shift_matrix(full, ghost + c - 1, begin, x_cells) for c in range(3)])
            for ghost in (below, 0, above)
        ]
    )
    turn = jnp.stack([shift_matrix(full, offset, 0, full) for offset in (1, 0, -1, -shift, shift)])
    vmem = pl.BlockSpec(memory_space=pltpu.VMEM)
    cells = planes * yl * x_cells
    dma = pltpu.SemaphoreType.DMA
    features, grad_in, weight_grad = pl.pallas_call(
        functools.partial(layer_kernel, n, nch, yl, scale),
        out_shape=(
            jax.ShapeDtypeStruct((local_ch, cells), BF16),
            jax.ShapeDtypeStruct((local_ch, cells), BF16),
            jax.ShapeDtypeStruct((27, local_ch, amount), F32),
        ),
        in_specs=[vmem] * 5,
        out_specs=(vmem,) * 3,
        scratch_shapes=[
            pltpu.VMEM((n, 2, nch + 1, planes * yl, local_ch, x_cells), BF16),
            pltpu.VMEM((amount, planes * (ny + 2) * full), BF16),
            pltpu.VMEM((3, local_ch, planes * ny * full), BF16),
            pltpu.VMEM((3, amount, planes * (yl + 2) * x_cells), BF16),
            pltpu.VMEM((3, local_ch, planes * (yl + 2) * x_cells), BF16),
            pltpu.VMEM((nch, local_ch, cells), F32),
            pltpu.VMEM((nch, local_ch, cells), F32),
            dma((2,)),
            dma((2, n, 2)),
            dma((2, n, 2)),
            dma((2,)),
            dma((2,)),
            dma((n, nch, 2)),
            dma((n, nch, 2)),
            dma((n, nch + 1, 2)),
            dma((n, nch + 1, 2)),
            dma((nch,)),
            dma((nch,)),
        ],
        compiler_params=pltpu.CompilerParams(
            collective_id=0, has_side_effects=True, vmem_limit_bytes=LIMIT
        ),
        name="layer",
    )(pieces(activations), pieces(cotangent), weight, near, turn)
    shape = (local_ch, planes, yl, x_cells)
    return (features.reshape(shape), grad_in.reshape(shape), weight_grad)


def solution(mesh):
    return jax.shard_map(
        on_device,
        mesh=mesh,
        in_specs=(
            P("ch", "grp", "gy", "gx"),
            P(None, "ch", None),
            P("ch", "grp", "gy", "gx"),
            P("grp"),
        ),
        out_specs=(P("ch", "grp", "gy", "gx"), P("ch", "grp", "gy", "gx"), P("grp", "ch", None)),
        check_vma=False,
    )
```

```python
import functools

import jax
import jax.numpy as jnp
from jax import lax
from jax.experimental import pallas as pl
from jax.experimental.pallas import tpu as pltpu
from jax.sharding import PartitionSpec as P

BF16 = jnp.bfloat16
F32 = jnp.float32

MESH = pl.DeviceIdType.MESH


def layer_kernel(
    n, nch, yl, scale,
    shear_ref, a_ref, t_ref, w_ref,
    f_ref, g_ref, wg_ref,
    buf, ext, rolled, ax, tx, term, arrived, near, turn,
    zs_sem, zr_sem, hs_sem, hr_sem, xs_sem, xr_sem, cs_sem, cr_sem, gs_sem, gr_sem,
):
    q = lax.axis_index("gy")
    h = lax.axis_index("ch")
    c = lax.axis_index("gx")
    other = 1 - c
    local_ch = w_ref.shape[1]
    amount = w_ref.shape[2]
    x_cells = buf.shape[-1]
    row = 2 * x_cells
    ny = n * yl
    plane = (ny + 2) * row
    flat = ny * row
    width = yl * x_cells
    span = (yl + 2) * x_cells
    valid = [(a, z, z + a - 1) for a in range(3) for z in range(2) if 0 <= z + a - 1 < 2]

    whole = (0, 2 * yl)
    halo = {"bottom": (2 * yl - 2, 2), "top": (0, 2)}
    rest = {"bottom": (0, 2 * yl - 2), "top": (2, 2 * yl - 2)}
    ends = {"bottom": (q == 0, n - 1), "top": (q == n - 1, 0)}

    def copy(slot, to, send, recv):
        return pltpu.make_async_remote_copy(
            src_ref=slot, dst_ref=slot, send_sem=send, recv_sem=recv, device_id=to, device_id_type=MESH
        )

    def channel(kind):
        return h if kind == 0 else nch

    def z_copy(step, direction, kind, source, part=whole):
        return copy(
            buf.at[source, c, channel(kind), pl.ds(*part)],
            {"gy": q - 1 if direction == 0 else q + 1},
            zs_sem.at[direction, step, kind],
            zr_sem.at[direction, step, kind],
        )

    def h_copy(kind, source, part, to):
        return copy(
            buf.at[source, c, channel(kind), pl.ds(*part)], {"gy": to}, hs_sem.at[kind], hr_sem.at[kind]
        )

    def x_copy(source, d, part=whole, sub=0, arrival=False):
        panel = lax.rem(h - d + nch, nch) if arrival else h
        return copy(
            buf.at[source, c, panel, pl.ds(*part)],
            {"ch": lax.rem(h + d, nch)},
            xs_sem.at[source, d, sub],
            xr_sem.at[source, d, sub],
        )

    def c_copy(source, d, part=whole, sub=0, side=None):
        kind = nch if d == nch else lax.rem(h - d + nch, nch)
        return copy(
            buf.at[source, c if side is None else side, kind, pl.ds(*part)],
            {"gx": other},
            cs_sem.at[source, d, sub],
            cr_sem.at[source, d, sub],
        )

    def pass_on(source, kind, part=whole, sub=0):
        if kind == 0:
            for d in range(1, nch):
                x_copy(source, d, part, sub).start()
            c_copy(source, 0, part, sub).start()
        else:
            c_copy(source, nch, part, sub).start()

    def relay(source, part=whole, sub=0):
        for d in range(1, nch):
            x_copy(source, d, part, sub, True).wait_recv()
            c_copy(source, d, part, sub).start()

    def from_core(source, kinds, part=whole, sub=0):
        for d in kinds:
            c_copy(source, d, part, sub, other).wait_recv()

    fields = range(nch)

    def each(step, body):
        if step < n - 1:

            @pl.when(q + step < n)
            def _():
                body(0, q + step, whole)

            @pl.when(q - step >= 0)
            def _():
                body(1, q - step, whole)
        else:
            for direction, name in ((0, "bottom"), (1, "top")):

                @pl.when(ends[name][0])
                def _(direction=direction, name=name):
                    body(direction, ends[name][1], rest[name])

    def onward(step, direction, kind, source):
        def go(part):
            z_copy(step, direction, kind, source, part).start()

        last = step == n - 2
        if direction == 0:

            @pl.when(q >= 1)
            def _():
                go(rest["bottom"] if last else whole)
        else:

            @pl.when(q < n - 1)
            def _():
                go(rest["top"] if last else whole)

    barrier = pltpu.get_barrier_semaphore()

    def greet(to):
        pl.semaphore_signal(barrier, inc=1, device_id=to, device_id_type=MESH)

    @pl.when(q > 0)
    def _():
        greet({"gy": q - 1})

    @pl.when(q < n - 1)
    def _():
        greet({"gy": q + 1})

    for name in ("bottom", "top"):

        @pl.when(ends[name][0])
        def _(name=name):
            greet({"gy": ends[name][1]})

    for d in range(1, nch):
        greet({"ch": lax.rem(h + d, nch)})
    greet({"gx": other})
    for field, kind in ((a_ref, h), (t_ref, nch)):
        for z in range(2):
            both = field[:, z].astype(F32)
            for y in range(yl):
                buf[q, c, kind, 2 * y + z] = both[:, y].astype(BF16)
    pl.semaphore_wait(barrier, 2 + nch)

    for kind in (1, 0):

        @pl.when(q == 0)
        def _(kind=kind):
            h_copy(kind, 0, halo["top"], n - 1).start()

        @pl.when(q == n - 1)
        def _(kind=kind):
            h_copy(kind, n - 1, halo["bottom"], 0).start()

    for kind in range(2):
        for direction in range(2):
            onward(0, direction, kind, q)
        pass_on(q, kind)

    def take(step):
        for kind in range(2):

            def body(direction, source, part, kind=kind):
                z_copy(step - 1, direction, kind, source, part).wait_recv()
                if step < n - 1:
                    onward(step, direction, kind, source)
                pass_on(source, kind, part)

            each(step, body)

    shift = shear_ref[0]

    def shift_matrix(offset, count):
        source = lax.broadcasted_iota(jnp.int32, (row, count), 1) + lax.rem(offset + 2 * row, row)
        source = jnp.where(source >= row, source - row, source)
        found = lax.broadcasted_iota(jnp.int32, (row, count), 0) == source
        return jnp.where(found, 1.0, 0.0).astype(BF16)

    for side, ghost in enumerate((jnp.where(q == 0, -shift, 0), 0, jnp.where(q == n - 1, shift, 0))):
        for s in range(3):
            near[side, s] = shift_matrix(ghost + c * x_cells + s - 1, x_cells)
    for k, offset in enumerate((1, 0, -1, -shift, shift)):
        turn[k] = shift_matrix(offset, row)

    take(1)
    for name in ("bottom", "top"):

        @pl.when(ends[name][0])
        def _(name=name):
            source, part = ends[name][1], halo[name]
            for kind in (1, 0):
                h_copy(kind, source, part, source).wait_recv()
                pass_on(source, kind, part, 1)

    relay(q)

    from_core(q, (nch,))
    each(1, lambda direction, source, part: from_core(source, (nch,), part))
    for name in ("bottom", "top"):

        @pl.when(ends[name][0])
        def _(name=name):
            from_core(ends[name][1], (nch,), halo[name], 1)

    def surround(field):
        out = ax if field == 0 else tx
        for r in range(yl + 2):
            if r == 0:
                source, y, side = lax.rem(q + n - 1, n), yl - 1, 0
            elif r == yl + 1:
                source, y, side = lax.rem(q + 1, n), 0, 2
            else:
                source, y, side = q, r - 1, 1
            for z in range(2):
                at = (z * (yl + 2) + r) * x_cells
                halves = [
                    buf[source, k, :nch, 2 * y + z].reshape(amount, x_cells)
                    if field == 0
                    else buf[source, k, nch, 2 * y + z]
                    for k in range(2)
                ]
                for s in range(3):
                    moved = jnp.dot(
                        halves[0], near[side, s, :x_cells], preferred_element_type=F32
                    ) + jnp.dot(halves[1], near[side, s, x_cells:], preferred_element_type=F32)
                    out[s, :, at : at + x_cells] = moved.astype(BF16)

    surround(1)

    def grad_step(b, carry):
        out = list(carry)
        for a, z, zz in valid:
            for s in range(3):
                window = tx[s, :, pl.ds(pl.multiple_of(zz * span + b * x_cells, x_cells), width)]
                out[z] += lax.dot_general(
                    w_ref[9 * (2 - a) + 3 * (2 - b) + 2 - s],
                    window,
                    (((0,), (0,)), ((), ())),
                    preferred_element_type=F32,
                )
        return tuple(out)

    planes = lax.fori_loop(0, 3, grad_step, (jnp.zeros((amount, width), F32),) * 2)
    for z in range(2):
        term[:, :, z * width : (z + 1) * width] = planes[z].reshape(nch, local_ch, width)

    each(1, lambda direction, source, part: relay(source, part))
    for name in ("bottom", "top"):

        @pl.when(ends[name][0])
        def _(name=name):
            relay(ends[name][1], halo[name], 1)

    def g_copy(d):
        to = lax.rem(h + d, nch)
        return pltpu.make_async_remote_copy(
            src_ref=term.at[to],
            dst_ref=arrived.at[d],
            send_sem=gs_sem.at[d],
            recv_sem=gr_sem.at[d],
            device_id={"ch": to},
            device_id_type=MESH,
        )

    for step in range(2, n - 1):
        take(step)
        if step == 2:
            for d in range(1, nch):
                g_copy(d).start()
        if step > 2:
            each(step - 1, lambda direction, source, part: relay(source, part))

    from_core(q, fields)
    each(1, lambda direction, source, part: from_core(source, fields, part))
    for name in ("bottom", "top"):

        @pl.when(ends[name][0])
        def _(name=name):
            from_core(ends[name][1], fields, halo[name], 1)

    surround(0)

    def rows_apart(flat_rows):
        return jnp.stack([flat_rows[:, y * x_cells : (y + 1) * x_cells] for y in range(yl)], axis=1)

    def features_step(b, carry):
        out = list(carry)
        for a, z, zz in valid:
            for s in range(3):
                window = ax[s, :, pl.ds(pl.multiple_of(zz * span + b * x_cells, x_cells), width)]
                out[z] += jnp.dot(w_ref[9 * a + 3 * b + s], window, preferred_element_type=F32)
        return tuple(out)

    planes = lax.fori_loop(0, 3, features_step, (jnp.zeros((local_ch, width), F32),) * 2)
    for z in range(2):
        f_ref[:, z] = rows_apart(planes[z]).astype(BF16)

    if n > 3:
        each(n - 2, lambda direction, source, part: relay(source, part))
    for step in range(2, n - 1):
        each(
            step, lambda direction, source, part: from_core(source, range(nch + 1), part)
        )

    late = jnp.where(2 * q < n, n - 1, 0)
    base = jnp.where(2 * q < n, 0, 1)

    def lay_out(source):
        for z in range(2):
            for y in range(yl):
                at = pl.multiple_of(z * plane + (1 + source * yl + y) * row, row)
                to = pl.multiple_of(z * flat + (source * yl + y) * row, row)
                for k in range(2):
                    ext[:, pl.ds(at + k * x_cells, x_cells)] = buf[source, k, :nch, 2 * y + z].reshape(
                        amount, x_cells
                    )
                    rolled[1, :, pl.ds(to + k * x_cells, x_cells)] = buf[source, k, nch, 2 * y + z]
                line = rolled[1, :, pl.ds(to, row)]
                for s in (0, 2):
                    rolled[s, :, pl.ds(to, row)] = jnp.dot(
                        line, turn[s], preferred_element_type=F32
                    ).astype(BF16)

    @pl.loop(0, n - 1)
    def _(k):
        lay_out(base + k)

    def products(a, b, start, rows):
        total = None
        for a_of, z, zz in valid:
            if a_of != a:
                continue
            left = rolled[:, :, pl.ds(pl.multiple_of(z * flat + start * row, row), rows * row)]
            right = ext[:, pl.ds(pl.multiple_of(zz * plane + (start + b) * row, row), rows * row)]
            part = lax.dot_general(
                left.reshape(3 * local_ch, rows * row),
                right,
                (((1,), (1,)), ((), ())),
                preferred_element_type=F32,
            )
            total = part if total is None else total + part
        return (total * scale).reshape(3, local_ch, amount)

    def early(a):
        many = (n - 1) * yl
        first = base * yl
        for b in range(3):
            at = 9 * a + 3 * b
            if b == 1:
                wg_ref[at : at + 3] = products(a, b, first, many)
            else:
                wg_ref[at : at + 3] = products(a, b, first + (1 if b == 0 else 0), many - 1)

    early(0)
    early(2)
    take(n - 1)
    early(1)
    each(n - 1, lambda direction, source, part: relay(source, part))
    for d in range(1, nch):
        g_copy(d).wait_recv()
    total = term[h]
    for d in range(1, nch):
        total = total + arrived[d]
    for z in range(2):
        g_ref[:, z] = rows_apart(total[:, z * width : (z + 1) * width]).astype(BF16)
    each(n - 1, lambda direction, source, part: from_core(source, range(nch + 1), part))

    lay_out(late)
    for z in range(2):
        first = ext[:, z * plane + row : z * plane + 2 * row]
        last = ext[:, z * plane + ny * row : z * plane + (ny + 1) * row]
        ext[:, z * plane : z * plane + row] = jnp.dot(
            last, turn[3], preferred_element_type=F32
        ).astype(BF16)
        ext[:, z * plane + (ny + 1) * row : (z + 1) * plane] = jnp.dot(
            first, turn[4], preferred_element_type=F32
        ).astype(BF16)

    for a in range(3):
        for b in range(3):
            at = 9 * a + 3 * b
            more = products(a, b, late * yl, yl)
            if b == 0:
                more = more + products(a, b, lax.rem(late * yl + yl, ny), 1)
            if b == 2:
                more = more + products(a, b, lax.rem(late * yl + ny - 1, ny), 1)
            wg_ref[at : at + 3] += more

    for step in range(n - 1):
        for kind in range(2):
            last = step == n - 2

            @pl.when((q >= 1) & (q + step < n))
            def _():
                z_copy(step, 0, kind, q + step, rest["bottom"] if last else whole).wait_send()

            @pl.when((q < n - 1) & (q - step >= 0))
            def _():
                z_copy(step, 1, kind, q - step, rest["top"] if last else whole).wait_send()

    def gone(source, part=whole, sub=0):
        for d in range(1, nch):
            x_copy(source, d, part, sub).wait_send()
        for d in range(nch + 1):
            c_copy(source, d, part, sub).wait_send()

    gone(q)
    for step in range(1, n):
        each(step, lambda direction, source, part: gone(source, part))
    for name, mine in (("bottom", "top"), ("top", "bottom")):

        @pl.when(ends[name][0])
        def _(name=name, mine=mine):
            gone(ends[name][1], halo[name], 1)
            for kind in range(2):
                h_copy(kind, q, halo[mine], ends[name][1]).wait_send()

    for d in range(1, nch):
        g_copy(d).wait_send()


def on_device(activations, weight, cotangent, shear_shift):
    local_ch, planes, yl, x_cells = activations.shape
    n = lax.axis_size("gy")
    nch = lax.axis_size("ch")
    amount = weight.shape[2]
    full = 2 * x_cells
    ny = n * yl
    scale = float(planes * ny * full) ** (-0.5)

    vmem = pl.BlockSpec(memory_space=pltpu.VMEM)
    cells = planes * yl * x_cells
    dma = pltpu.SemaphoreType.DMA
    blocks = n * 2 * (nch + 1) * 2 * yl * local_ch * x_cells
    whole = planes * (ny + 2) * full * (amount + 3 * local_ch)
    around = 3 * (amount + local_ch) * planes * (yl + 2) * x_cells
    held = 2 * (blocks + whole + around) + 8 * amount * cells + 27 * local_ch * amount * 6
    limit = min(held + 14 * 2**20, 60 * 2**20)
    features, grad_in, weight_grad = pl.pallas_call(
        functools.partial(layer_kernel, n, nch, yl, scale),
        out_shape=(
            jax.ShapeDtypeStruct(activations.shape, BF16),
            jax.ShapeDtypeStruct(activations.shape, BF16),
            jax.ShapeDtypeStruct((27, local_ch, amount), F32),
        ),
        in_specs=[pl.BlockSpec(memory_space=pltpu.SMEM)] + [vmem] * 3,
        out_specs=(vmem,) * 3,
        scratch_shapes=[
            pltpu.VMEM((n, 2, nch + 1, planes * yl, local_ch, x_cells), BF16),
            pltpu.VMEM((amount, planes * (ny + 2) * full), BF16),
            pltpu.VMEM((3, local_ch, planes * ny * full), BF16),
            pltpu.VMEM((3, amount, planes * (yl + 2) * x_cells), BF16),
            pltpu.VMEM((3, local_ch, planes * (yl + 2) * x_cells), BF16),
            pltpu.VMEM((nch, local_ch, cells), F32),
            pltpu.VMEM((nch, local_ch, cells), F32),
            pltpu.VMEM((3, 3, full, x_cells), BF16),
            pltpu.VMEM((5, full, full), BF16),
            dma((2, n, 2)),
            dma((2, n, 2)),
            dma((2,)),
            dma((2,)),
            dma((n, nch, 2)),
            dma((n, nch, 2)),
            dma((n, nch + 1, 2)),
            dma((n, nch + 1, 2)),
            dma((nch,)),
            dma((nch,)),
        ],
        compiler_params=pltpu.CompilerParams(
            collective_id=0, has_side_effects=True, vmem_limit_bytes=limit
        ),
        name="layer",
    )(shear_shift, activations, cotangent, weight)
    return (features, grad_in, weight_grad)


def solution(mesh):
    return jax.shard_map(
        on_device,
        mesh=mesh,
        in_specs=(
            P("ch", "grp", "gy", "gx"),
            P(None, "ch", None),
            P("ch", "grp", "gy", "gx"),
            P("grp"),
        ),
        out_specs=(P("ch", "grp", "gy", "gx"), P("ch", "grp", "gy", "gx"), P("grp", "ch", None)),
        check_vma=False,
    )
```

```python
import functools

import jax
import jax.numpy as jnp
from jax import lax
from jax.experimental import pallas as pl
from jax.experimental.pallas import tpu as pltpu
from jax.sharding import PartitionSpec as P

BF16 = jnp.bfloat16
F32 = jnp.float32

MESH = pl.DeviceIdType.MESH


def layer_kernel(
    n, nch, yl, scale,
    shear_ref, a_ref, t_ref, w_ref,
    f_ref, g_ref, wg_ref,
    buf, ext, rolled, ax, tx, term, arrived, near, turn,
    zs_sem, zr_sem, hs_sem, hr_sem, xs_sem, xr_sem, cs_sem, cr_sem, gs_sem, gr_sem,
):
    q = lax.axis_index("gy")
    h = lax.axis_index("ch")
    c = lax.axis_index("gx")
    other = 1 - c
    local_ch = w_ref.shape[1]
    amount = w_ref.shape[2]
    x_cells = buf.shape[-1]
    row = 2 * x_cells
    ny = n * yl
    plane = (ny + 2) * row
    flat = ny * row
    width = yl * x_cells
    span = (yl + 2) * x_cells
    valid = [(a, z, z + a - 1) for a in range(3) for z in range(2) if 0 <= z + a - 1 < 2]

    whole = (0, 2 * yl)
    halo = {"bottom": (2 * yl - 2, 2), "top": (0, 2)}
    rest = {"bottom": (0, 2 * yl - 2), "top": (2, 2 * yl - 2)}
    ends = {"bottom": (q == 0, n - 1), "top": (q == n - 1, 0)}

    def copy(slot, to, send, recv):
        return pltpu.make_async_remote_copy(
            src_ref=slot, dst_ref=slot, send_sem=send, recv_sem=recv, device_id=to, device_id_type=MESH
        )

    def channel(kind):
        return h if kind == 0 else nch

    def z_copy(step, direction, kind, source, part=whole):
        return copy(
            buf.at[source, c, channel(kind), pl.ds(*part)],
            {"gy": q - 1 if direction == 0 else q + 1},
            zs_sem.at[direction, step, kind],
            zr_sem.at[direction, step, kind],
        )

    def h_copy(kind, source, part, to):
        return copy(
            buf.at[source, c, channel(kind), pl.ds(*part)], {"gy": to}, hs_sem.at[kind], hr_sem.at[kind]
        )

    def x_copy(source, d, part=whole, sub=0, arrival=False):
        panel = lax.rem(h - d + nch, nch) if arrival else h
        return copy(
            buf.at[source, c, panel, pl.ds(*part)],
            {"ch": lax.rem(h + d, nch)},
            xs_sem.at[source, d, sub],
            xr_sem.at[source, d, sub],
        )

    def c_copy(source, d, part=whole, sub=0, side=None):
        kind = nch if d == nch else lax.rem(h - d + nch, nch)
        return copy(
            buf.at[source, c if side is None else side, kind, pl.ds(*part)],
            {"gx": other},
            cs_sem.at[source, d, sub],
            cr_sem.at[source, d, sub],
        )

    def pass_on(source, kind, part=whole, sub=0):
        if kind == 0:
            for d in range(1, nch):
                x_copy(source, d, part, sub).start()
            c_copy(source, 0, part, sub).start()
        else:
            c_copy(source, nch, part, sub).start()

    def relay(source, part=whole, sub=0):
        for d in range(1, nch):
            x_copy(source, d, part, sub, True).wait_recv()
            c_copy(source, d, part, sub).start()

    def from_core(source, kinds, part=whole, sub=0):
        for d in kinds:
            c_copy(source, d, part, sub, other).wait_recv()

    fields = range(nch)

    def each(step, body):
        if step < n - 1:

            @pl.when(q + step < n)
            def _():
                body(0, q + step, whole)

            @pl.when(q - step >= 0)
            def _():
                body(1, q - step, whole)
        else:
            for direction, name in ((0, "bottom"), (1, "top")):

                @pl.when(ends[name][0])
                def _(direction=direction, name=name):
                    body(direction, ends[name][1], rest[name])

    def onward(step, direction, kind, source):
        def go(part):
            z_copy(step, direction, kind, source, part).start()

        last = step == n - 2
        if direction == 0:

            @pl.when(q >= 1)
            def _():
                go(rest["bottom"] if last else whole)
        else:

            @pl.when(q < n - 1)
            def _():
                go(rest["top"] if last else whole)

    barrier = pltpu.get_barrier_semaphore()

    def greet(to):
        pl.semaphore_signal(barrier, inc=1, device_id=to, device_id_type=MESH)

    @pl.when(q > 0)
    def _():
        greet({"gy": q - 1})

    @pl.when(q < n - 1)
    def _():
        greet({"gy": q + 1})

    for name in ("bottom", "top"):

        @pl.when(ends[name][0])
        def _(name=name):
            greet({"gy": ends[name][1]})

    for d in range(1, nch):
        greet({"ch": lax.rem(h + d, nch)})
    greet({"gx": other})
    for field, kind in ((a_ref, h), (t_ref, nch)):
        for z in range(2):
            both = field[:, z].astype(F32)
            for y in range(yl):
                buf[q, c, kind, 2 * y + z] = both[:, y].astype(BF16)
    pl.semaphore_wait(barrier, 2 + nch)

    for kind in (1, 0):

        @pl.when(q == 0)
        def _(kind=kind):
            h_copy(kind, 0, halo["top"], n - 1).start()

        @pl.when(q == n - 1)
        def _(kind=kind):
            h_copy(kind, n - 1, halo["bottom"], 0).start()

    for kind in range(2):
        for direction in range(2):
            onward(0, direction, kind, q)
        pass_on(q, kind)

    def take(step):
        for kind in range(2):

            def body(direction, source, part, kind=kind):
                z_copy(step - 1, direction, kind, source, part).wait_recv()
                if step < n - 1:
                    onward(step, direction, kind, source)
                pass_on(source, kind, part)

            each(step, body)

    shift = shear_ref[0]

    def shift_matrix(offset, count):
        source = lax.broadcasted_iota(jnp.int32, (row, count), 1) + lax.rem(offset + 2 * row, row)
        source = jnp.where(source >= row, source - row, source)
        found = lax.broadcasted_iota(jnp.int32, (row, count), 0) == source
        return jnp.where(found, 1.0, 0.0).astype(BF16)

    for side, ghost in enumerate((jnp.where(q == 0, -shift, 0), 0, jnp.where(q == n - 1, shift, 0))):
        for s in range(3):
            near[side, s] = shift_matrix(ghost + c * x_cells + s - 1, x_cells)
    for k, offset in enumerate((1, 0, -1, -shift, shift)):
        turn[k] = shift_matrix(offset, row)

    take(1)
    for name in ("bottom", "top"):

        @pl.when(ends[name][0])
        def _(name=name):
            source, part = ends[name][1], halo[name]
            for kind in (1, 0):
                h_copy(kind, source, part, source).wait_recv()
                pass_on(source, kind, part, 1)

    relay(q)

    from_core(q, (nch,))
    each(1, lambda direction, source, part: from_core(source, (nch,), part))
    for name in ("bottom", "top"):

        @pl.when(ends[name][0])
        def _(name=name):
            from_core(ends[name][1], (nch,), halo[name], 1)

    def surround(field):
        out = ax if field == 0 else tx
        for r in range(yl + 2):
            if r == 0:
                source, y, side = lax.rem(q + n - 1, n), yl - 1, 0
            elif r == yl + 1:
                source, y, side = lax.rem(q + 1, n), 0, 2
            else:
                source, y, side = q, r - 1, 1
            for z in range(2):
                at = (z * (yl + 2) + r) * x_cells
                halves = [
                    buf[source, k, :nch, 2 * y + z].reshape(amount, x_cells)
                    if field == 0
                    else buf[source, k, nch, 2 * y + z]
                    for k in range(2)
                ]
                for s in range(3):
                    moved = jnp.dot(
                        halves[0], near[side, s, :x_cells], preferred_element_type=F32
                    ) + jnp.dot(halves[1], near[side, s, x_cells:], preferred_element_type=F32)
                    out[s, :, at : at + x_cells] = moved.astype(BF16)

    surround(1)

    def grad_step(b, carry):
        out = list(carry)
        for a, z, zz in valid:
            for s in range(3):
                window = tx[s, :, pl.ds(pl.multiple_of(zz * span + b * x_cells, x_cells), width)]
                out[z] += lax.dot_general(
                    w_ref[9 * (2 - a) + 3 * (2 - b) + 2 - s],
                    window,
                    (((0,), (0,)), ((), ())),
                    preferred_element_type=F32,
                )
        return tuple(out)

    planes = lax.fori_loop(0, 3, grad_step, (jnp.zeros((amount, width), F32),) * 2)
    for z in range(2):
        term[:, :, z * width : (z + 1) * width] = planes[z].reshape(nch, local_ch, width)

    each(1, lambda direction, source, part: relay(source, part))
    for name in ("bottom", "top"):

        @pl.when(ends[name][0])
        def _(name=name):
            relay(ends[name][1], halo[name], 1)

    def g_copy(d):
        to = lax.rem(h + d, nch)
        return pltpu.make_async_remote_copy(
            src_ref=term.at[to],
            dst_ref=arrived.at[d],
            send_sem=gs_sem.at[d],
            recv_sem=gr_sem.at[d],
            device_id={"ch": to},
            device_id_type=MESH,
        )

    for step in range(2, n - 1):
        take(step)
        if step == 2:
            for d in range(1, nch):
                g_copy(d).start()
        if step > 2:
            each(step - 1, lambda direction, source, part: relay(source, part))

    from_core(q, fields)
    each(1, lambda direction, source, part: from_core(source, fields, part))
    for name in ("bottom", "top"):

        @pl.when(ends[name][0])
        def _(name=name):
            from_core(ends[name][1], fields, halo[name], 1)

    surround(0)

    def rows_apart(flat_rows):
        return jnp.stack([flat_rows[:, y * x_cells : (y + 1) * x_cells] for y in range(yl)], axis=1)

    def features_step(b, carry):
        out = list(carry)
        for a, z, zz in valid:
            for s in range(3):
                window = ax[s, :, pl.ds(pl.multiple_of(zz * span + b * x_cells, x_cells), width)]
                out[z] += jnp.dot(w_ref[9 * a + 3 * b + s], window, preferred_element_type=F32)
        return tuple(out)

    planes = lax.fori_loop(0, 3, features_step, (jnp.zeros((local_ch, width), F32),) * 2)
    for z in range(2):
        f_ref[:, z] = rows_apart(planes[z]).astype(BF16)

    if n > 3:
        each(n - 2, lambda direction, source, part: relay(source, part))
    for step in range(2, n - 1):
        each(
            step, lambda direction, source, part: from_core(source, range(nch + 1), part)
        )

    late = jnp.where(2 * q < n, n - 1, 0)
    base = jnp.where(2 * q < n, 0, 1)

    def lay_out(source):
        for z in range(2):
            for y in range(yl):
                at = pl.multiple_of(z * plane + (1 + source * yl + y) * row, row)
                to = pl.multiple_of(z * flat + (source * yl + y) * row, row)
                for k in range(2):
                    ext[:, pl.ds(at + k * x_cells, x_cells)] = buf[source, k, :nch, 2 * y + z].reshape(
                        amount, x_cells
                    )
                    rolled[1, :, pl.ds(to + k * x_cells, x_cells)] = buf[source, k, nch, 2 * y + z]
                line = rolled[1, :, pl.ds(to, row)]
                for s in (0, 2):
                    rolled[s, :, pl.ds(to, row)] = jnp.dot(
                        line, turn[s], preferred_element_type=F32
                    ).astype(BF16)

    @pl.loop(0, n - 1)
    def _(k):
        lay_out(base + k)

    def products(a, b, start, rows):
        total = None
        for a_of, z, zz in valid:
            if a_of != a:
                continue
            left = rolled[:, :, pl.ds(pl.multiple_of(z * flat + start * row, row), rows * row)]
            right = ext[:, pl.ds(pl.multiple_of(zz * plane + (start + b) * row, row), rows * row)]
            part = lax.dot_general(
                left.reshape(3 * local_ch, rows * row),
                right,
                (((1,), (1,)), ((), ())),
                preferred_element_type=F32,
            )
            total = part if total is None else total + part
        return (total * scale).reshape(3, local_ch, amount)

    def early(a):
        many = (n - 1) * yl
        first = base * yl
        for b in range(3):
            at = 9 * a + 3 * b
            if b == 1:
                wg_ref[at : at + 3] = products(a, b, first, many)
            else:
                wg_ref[at : at + 3] = products(a, b, first + (1 if b == 0 else 0), many - 1)

    early(0)
    early(2)
    take(n - 1)
    early(1)
    each(n - 1, lambda direction, source, part: relay(source, part))
    for d in range(1, nch):
        g_copy(d).wait_recv()
    total = term[h]
    for d in range(1, nch):
        total = total + arrived[d]
    for z in range(2):
        g_ref[:, z] = rows_apart(total[:, z * width : (z + 1) * width]).astype(BF16)
    each(n - 1, lambda direction, source, part: from_core(source, range(nch + 1), part))

    lay_out(late)
    for z in range(2):
        first = ext[:, z * plane + row : z * plane + 2 * row]
        last = ext[:, z * plane + ny * row : z * plane + (ny + 1) * row]
        ext[:, z * plane : z * plane + row] = jnp.dot(
            last, turn[3], preferred_element_type=F32
        ).astype(BF16)
        ext[:, z * plane + (ny + 1) * row : (z + 1) * plane] = jnp.dot(
            first, turn[4], preferred_element_type=F32
        ).astype(BF16)

    for a in range(3):
        for b in range(3):
            at = 9 * a + 3 * b
            more = products(a, b, late * yl, yl)
            if b == 0:
                more = more + products(a, b, lax.rem(late * yl + yl, ny), 1)
            if b == 2:
                more = more + products(a, b, lax.rem(late * yl + ny - 1, ny), 1)
            wg_ref[at : at + 3] += more

    for step in range(n - 1):
        for kind in range(2):
            last = step == n - 2

            @pl.when((q >= 1) & (q + step < n))
            def _():
                z_copy(step, 0, kind, q + step, rest["bottom"] if last else whole).wait_send()

            @pl.when((q < n - 1) & (q - step >= 0))
            def _():
                z_copy(step, 1, kind, q - step, rest["top"] if last else whole).wait_send()

    def gone(source, part=whole, sub=0):
        for d in range(1, nch):
            x_copy(source, d, part, sub).wait_send()
        for d in range(nch + 1):
            c_copy(source, d, part, sub).wait_send()

    gone(q)
    for step in range(1, n):
        each(step, lambda direction, source, part: gone(source, part))
    for name, mine in (("bottom", "top"), ("top", "bottom")):

        @pl.when(ends[name][0])
        def _(name=name, mine=mine):
            gone(ends[name][1], halo[name], 1)
            for kind in range(2):
                h_copy(kind, q, halo[mine], ends[name][1]).wait_send()

    for d in range(1, nch):
        g_copy(d).wait_send()


def on_device(activations, weight, cotangent, shear_shift):
    local_ch, planes, yl, x_cells = activations.shape
    n = lax.axis_size("gy")
    nch = lax.axis_size("ch")
    amount = weight.shape[2]
    full = 2 * x_cells
    ny = n * yl
    scale = float(planes * ny * full) ** (-0.5)

    vmem = pl.BlockSpec(memory_space=pltpu.VMEM)
    cells = planes * yl * x_cells
    dma = pltpu.SemaphoreType.DMA
    blocks = n * 2 * (nch + 1) * 2 * yl * local_ch * x_cells
    whole = planes * (ny + 2) * full * (amount + 3 * local_ch)
    around = 3 * (amount + local_ch) * planes * (yl + 2) * x_cells
    held = 2 * (blocks + whole + around) + 8 * amount * cells + 27 * local_ch * amount * 6
    limit = min(held + 4 * 2**20, 60 * 2**20)
    features, grad_in, weight_grad = pl.pallas_call(
        functools.partial(layer_kernel, n, nch, yl, scale),
        out_shape=(
            jax.ShapeDtypeStruct(activations.shape, BF16),
            jax.ShapeDtypeStruct(activations.shape, BF16),
            jax.ShapeDtypeStruct((27, local_ch, amount), F32),
        ),
        in_specs=[pl.BlockSpec(memory_space=pltpu.SMEM)] + [vmem] * 3,
        out_specs=(vmem,) * 3,
        scratch_shapes=[
            pltpu.VMEM((n, 2, nch + 1, planes * yl, local_ch, x_cells), BF16),
            pltpu.VMEM((amount, planes * (ny + 2) * full), BF16),
            pltpu.VMEM((3, local_ch, planes * ny * full), BF16),
            pltpu.VMEM((3, amount, planes * (yl + 2) * x_cells), BF16),
            pltpu.VMEM((3, local_ch, planes * (yl + 2) * x_cells), BF16),
            pltpu.VMEM((nch, local_ch, cells), F32),
            pltpu.VMEM((nch, local_ch, cells), F32),
            pltpu.VMEM((3, 3, full, x_cells), BF16),
            pltpu.VMEM((5, full, full), BF16),
            dma((2, n, 2)),
            dma((2, n, 2)),
            dma((2,)),
            dma((2,)),
            dma((n, nch, 2)),
            dma((n, nch, 2)),
            dma((n, nch + 1, 2)),
            dma((n, nch + 1, 2)),
            dma((nch,)),
            dma((nch,)),
        ],
        compiler_params=pltpu.CompilerParams(
            collective_id=0, has_side_effects=True, vmem_limit_bytes=limit
        ),
        name="layer",
    )(shear_shift, activations, cotangent, weight)
    return (features, grad_in, weight_grad)


def solution(mesh):
    return jax.shard_map(
        on_device,
        mesh=mesh,
        in_specs=(
            P("ch", "grp", "gy", "gx"),
            P(None, "ch", None),
            P("ch", "grp", "gy", "gx"),
            P("grp"),
        ),
        out_specs=(P("ch", "grp", "gy", "gx"), P("ch", "grp", "gy", "gx"), P("grp", "ch", None)),
        check_vma=False,
    )
```
